32 devices in a mesh: section: 4 (over y, core), dp: 8 (over z, x).
Axes of the slice: x: 2, y: 2, z: 4, core: 2. Of those that a mesh axis runs over, the one named last changes fastest.
Arguments:
- w_in: bfloat16 [4, 5120, 4096], P('section', 'dp'), may hold values from -0.09375 to 0.09375
- w_out: bfloat16 [4, 5120, 4096], P('section', 'dp'), may hold values from -0.078125 to 0.078125
- input_stash: bfloat16 [4, 2, 128, 4096], P('section', None, 'dp'), may hold values from -6 to 6
- hidden_stash: bfloat16 [4, 2, 128, 5120], P('section', None, None, 'dp'), may hold values from -6 to 6
- gate_stash: float32 [4, 2, 128], P('section'), may hold values from 0.25 to 1
- block_pick: int32 [4, 2], P('section'), may hold values from 0 to 1
- slot_order: int32 [4, 2], P('section'), may hold values from 0 to 1, each once within a row
- arriving: bfloat16 [4, 2, 128, 4096], P('section', None, 'dp'), may hold values from -6 to 6
- loss_grads: bfloat16 [1, 2, 128, 4096], P(None, None, 'dp'), may hold values from -6 to 6
Outputs:
- passed: bfloat16 [4, 2, 2, 128, 4096], P('section', None, None, 'dp')
- grad_in: bfloat16 [4, 5120, 4096], P('section', 'dp')
- grad_out: bfloat16 [4, 5120, 4096], P('section', 'dp')
- gate_grads: float32 [4, 2, 128], P('section')
The draws below stay inside these ranges and needn't reach their ends.
Inputs may be any that keep to these rules, and one draw needn't show every extreme that they name: Each row of slot_order holds every slot 0 to 1 once.
All inputs are finite; a program needn't handle non-finite values.
Results may differ from the reference program's by a relative error of at most 0.0055.
Values may be sent and summed in bfloat16 or wider, within the bound.
No kernel may reach another device: no remote copies, remote signals or barrier semaphores. Data moves between devices by JAX's collectives and lax.ppermute only.
A program may use at most 128 MiB of HBM per device.

```python
import jax
import jax.numpy as jnp
from jax import lax

D = 4096
FW = 5120
BLK = 128
NBLK = 2
TICKS = 2
SECTIONS = 4


def plant(values, key, smallest, high):
    longest = values.shape.index(max(values.shape))
    spots = []
    for shift in (0, 1):
        where = [jax.random.randint(jax.random.fold_in(key, axis), (), 0, length) for axis, length in enumerate(values.shape)]
        where[longest] = (where[longest] + shift) % values.shape[longest]
        spots.append(tuple(where))
    return values.at[spots[0]].set(smallest).at[spots[1]].set(high)


def levels(rng, shape, shards, smallest, high):
    gain = 1.0
    for dim, shards_of in shards:
        heights = jax.random.uniform(jax.random.fold_in(jax.random.fold_in(rng, 6), dim), (shards_of,), jnp.float32, smallest / len(shards), high / len(shards))
        gain = gain * jnp.repeat(jnp.exp(heights), shape[dim] // shards_of).reshape((-1,) + (1,) * (len(shape) - 1 - dim))
    return gain


def centred(rng, dims, width, bound, split=(), kind=jnp.bfloat16):
    factor_of = levels(rng, dims, split, -0.22, 0.18) if split else 1.0
    array = jax.random.normal(rng, dims, jnp.float32) * width * factor_of
    return jnp.minimum(jnp.maximum(array, -bound), bound).astype(kind)


def setup_inputs(seed: int = 0) -> dict:
    keys = jax.random.split(jax.random.key(seed), 10)
    return {
        "w_in": centred(keys[0], (SECTIONS, FW, D), D ** -0.5, 0.09375, ((0, 4), (1, 8))),
        "w_out": centred(keys[1], (SECTIONS, FW, D), FW ** -0.5, 0.078125, ((0, 4), (1, 8))),
        "input_stash": centred(keys[2], (SECTIONS, TICKS, BLK, D), 1.0, 6.0, ((0, 4), (2, 8))),
        "hidden_stash": centred(keys[3], (SECTIONS, TICKS, BLK, FW), 1.0, 6.0, ((0, 4), (3, 8))),
        "gate_stash": jnp.clip(0.25 + 0.75 * jax.random.uniform(keys[4], (SECTIONS, TICKS, BLK), jnp.float32) ** levels(keys[4], (SECTIONS, TICKS, BLK), ((0, 4),), -0.2, 0.2), 0.25, 1.0),
        "block_pick": plant(jax.random.randint(keys[5], (SECTIONS, TICKS), 0, NBLK), jax.random.fold_in(keys[5], 1), 0, NBLK - 1).astype(jnp.int32),
        "slot_order": jax.vmap(lambda own: jax.random.permutation(own, TICKS))(jax.random.split(keys[6], SECTIONS)).reshape((SECTIONS, TICKS)).astype(jnp.int32),
        "arriving": centred(keys[7], (SECTIONS, NBLK, BLK, D), 1.0, 6.0, ((0, 4), (2, 8))),
        "loss_grads": centred(keys[8], (TICKS - 1, NBLK, BLK, D), 1.0, 6.0, ((2, 8),)),
    }


def section_tick(incoming, section, tick_index, w_in, w_out, input_stash, hidden_stash, gate_stash, block_pick, slot_order):
    slot_id = slot_order[section, tick_index]
    block_id = block_pick[section, slot_id]
    gate_vals = gate_stash[section, slot_id]
    pre_act = hidden_stash[section, slot_id]
    saved_rows = input_stash[section, slot_id]
    selected = incoming[block_id]
    upstream = lax.dot_general(selected, w_out[section], (((1,), (1,)), ((), ())), preferred_element_type=jnp.float32)
    active = jnp.maximum(pre_act.astype(jnp.float32), 0.0)
    hid_grad = jnp.where(pre_act > 0, upstream * gate_vals[:, None], 0.0).astype(jnp.bfloat16)
    expert_in = jnp.dot(hid_grad, w_in[section], preferred_element_type=jnp.float32)
    blocks = incoming.shape[0]
    placed = jnp.where((jnp.arange(blocks) == block_id)[:, None, None], expert_in[None], 0.0)
    updated = (incoming.astype(jnp.float32) + placed).astype(jnp.bfloat16)
    gate_part = jnp.sum(active * upstream, axis=1)
    weighted = (active * gate_vals[:, None]).astype(jnp.bfloat16)
    return updated, gate_part, selected, weighted, hid_grad, saved_rows


def reference(w_in, w_out, input_stash, hidden_stash, gate_stash, block_pick, slot_order, arriving, loss_grads):
    section_ids = jnp.arange(SECTIONS)
    incoming_all = arriving
    passed_list = []
    gate_list = []
    sel_list = []
    weigh_list = []
    hid_list = []
    save_list = []
    for tick_index in range(TICKS):
        def per_section(item):
            return section_tick(item[1], item[0], tick_index, w_in, w_out, input_stash, hidden_stash, gate_stash, block_pick, slot_order)
        updated, gate_part, selected, weighted, hid_grad, saved_rows = lax.map(per_section, (section_ids, incoming_all))
        passed_list.append(updated)
        gate_list.append(gate_part)
        sel_list.append(selected)
        weigh_list.append(weighted)
        hid_list.append(hid_grad)
        save_list.append(saved_rows)
        if tick_index + 1 < TICKS:
            incoming_all = jnp.concatenate([updated[1:], loss_grads[tick_index][None]], axis=0)
    passed = jnp.stack(passed_list, axis=1)
    sel_all = jnp.stack(sel_list, axis=1)
    weigh_all = jnp.stack(weigh_list, axis=1)
    hid_all = jnp.stack(hid_list, axis=1)
    save_all = jnp.stack(save_list, axis=1)
    contract = (((0,), (0,)), ((), ()))

    def grads_of(item):
        sel_rows, weigh_rows, hid_rows, save_rows = item
        out_grad = lax.dot_general(weigh_rows.reshape(-1, FW), sel_rows.reshape(-1, D), contract, preferred_element_type=jnp.float32)
        in_grad = lax.dot_general(hid_rows.reshape(-1, FW), save_rows.reshape(-1, D), contract, preferred_element_type=jnp.float32)
        return in_grad.astype(jnp.bfloat16), out_grad.astype(jnp.bfloat16)

    grad_in, grad_out = lax.map(grads_of, (sel_all, weigh_all, hid_all, save_all))
    gate_parts = jnp.stack(gate_list, axis=0)
    onehot = (slot_order[:, :, None] == jnp.arange(TICKS)[None, None, :]).astype(jnp.float32)
    gate_grads = jnp.einsum("stp,tsr->spr", onehot, gate_parts, precision=lax.Precision.HIGHEST)
    return passed, grad_in, grad_out, gate_grads
```

```python
import functools

import jax
import jax.numpy as jnp
from jax import lax
from jax.experimental import pallas as pl
from jax.experimental.pallas import tpu as pltpu
from jax.sharding import PartitionSpec as P

BF16 = jnp.bfloat16
F32 = jnp.float32
VMEM = pl.BlockSpec(memory_space=pltpu.VMEM)
SMEM = pl.BlockSpec(memory_space=pltpu.SMEM)
ANY = pl.BlockSpec(memory_space=pl.ANY)
PARAMS = pltpu.CompilerParams(vmem_limit_bytes=32 * 2**20)


def column_tile(width):
    return 512 if width % 512 == 0 else width


def expert_kernel(devices, inner, scalars, *refs):
    chunks = refs[:devices]
    w_out, w_in, hidden, gates = refs[devices : devices + 4]
    parts = refs[devices + 4 : 2 * devices + 4]
    rows_ref, weighted_ref, hid_ref, gate_ref, pre_ref, scale_ref = refs[2 * devices + 4 :]
    rows = chunks[0].shape[0]
    me, slot = scalars[0], scalars[1]
    for k in range(devices):
        own = pl.ds(k * rows, rows)
        rows_ref[own, :] = chunks[k][...]
        pre_ref[own, :] = hidden[slot, me ^ k]
        scale_ref[own, :] = gates[slot, me ^ k]
    upstream = lax.dot_general(
        rows_ref[...], w_out[...], (((1,), (1,)), ((), ())), preferred_element_type=F32
    )
    pre = pre_ref[...].astype(F32)
    scale = scale_ref[...]
    active = jnp.maximum(pre, 0.0)
    gate_sum = jnp.sum(active * upstream, axis=1, keepdims=True)
    weighted_ref[...] = (active * scale).astype(BF16)
    hid_grad = jnp.where(pre > 0, upstream * scale, 0.0).astype(BF16)
    outer = devices // inner
    for k in range(devices):
        peer = me ^ k
        gate_ref[peer] = gate_sum[k * rows : (k + 1) * rows]
        place = (peer % inner) * outer + peer // inner
        hid_ref[place] = hid_grad[k * rows : (k + 1) * rows]
    width = w_in.shape[1]
    tile = column_tile(width)
    for start in range(0, width, tile):
        cols = pl.ds(start, tile)
        part = jnp.dot(hid_grad, w_in[:, cols], preferred_element_type=F32).astype(BF16)
        for k in range(devices):
            parts[k][:, cols] = part[k * rows : (k + 1) * rows]


def expert(chunks, w_out, w_in, hidden, gates, scalars, inner):
    devices = len(chunks)
    rows, width = chunks[0].shape
    units = w_out.shape[0]
    tokens = devices * rows
    chunk = jax.ShapeDtypeStruct((rows, width), BF16)
    flops = 4 * tokens * units * width
    return pl.pallas_call(
        functools.partial(expert_kernel, devices, inner),
        in_specs=[SMEM] + [VMEM] * (devices + 4),
        out_specs=[VMEM] * (devices + 4),
        out_shape=[chunk] * devices
        + [
            jax.ShapeDtypeStruct((tokens, width), BF16),
            jax.ShapeDtypeStruct((tokens, units), BF16),
            jax.ShapeDtypeStruct((devices, rows, units), BF16),
            jax.ShapeDtypeStruct((devices, rows, 1), F32),
        ],
        scratch_shapes=[pltpu.VMEM((tokens, units), BF16), pltpu.VMEM((tokens, 1), F32)],
        compiler_params=PARAMS,
        cost_estimate=pl.CostEstimate(flops=flops, bytes_accessed=2 * 2**20, transcendentals=0),
        name="expert_tick",
    )(scalars, *chunks, w_out, w_in, hidden, gates)


def grads_kernel(ticks, slots, saved, *refs):
    rows_refs = refs[:ticks]
    weighted_refs = refs[ticks : 2 * ticks]
    hid_refs = refs[2 * ticks : 3 * ticks]
    grad_in, grad_out, hid_all, hid_t, weighted_t, in_buf, out_buf, sems = refs[3 * ticks :]
    devices, rows, units = hid_refs[0].shape
    tokens = devices * rows
    for t in range(ticks):
        for d in range(devices):
            hid_all[d * ticks + slots[0, t]] = hid_refs[t][d]
        weighted_t[:, t * tokens : (t + 1) * tokens] = weighted_refs[t][...].T
    hid_t[...] = hid_all[...].reshape(ticks * tokens, units).T
    width = grad_in.shape[1]
    tile = column_tile(width)
    steps = width // tile
    copies = []
    for step in range(steps):
        cols = pl.ds(step * tile, tile)
        buf = step % 2
        if step >= 2:
            for copy in copies[2 * (step - 2) : 2 * (step - 1)]:
                copy.wait()
        in_buf[buf] = jnp.dot(hid_t[...], saved[:, cols], preferred_element_type=F32).astype(BF16)
        first = pltpu.make_async_copy(in_buf.at[buf], grad_in.at[:, cols], sems.at[0, buf])
        first.start()
        total = jnp.dot(
            weighted_t[...],
            jnp.concatenate([ref[:, cols] for ref in rows_refs], axis=0),
            preferred_element_type=F32,
        )
        out_buf[buf] = total.astype(BF16)
        second = pltpu.make_async_copy(out_buf.at[buf], grad_out.at[:, cols], sems.at[1, buf])
        second.start()
        copies += [first, second]
    for copy in copies[2 * max(steps - 2, 0) :]:
        copy.wait()


def weight_grads(slots, saved, rows_list, weighted_list, hid_list):
    ticks = len(rows_list)
    tokens, width = rows_list[0].shape
    devices, rows, units = hid_list[0].shape
    tile = column_tile(width)
    out = jax.ShapeDtypeStruct((units, width), BF16)
    return pl.pallas_call(
        functools.partial(grads_kernel, ticks),
        in_specs=[SMEM] + [VMEM] * (3 * ticks + 1),
        out_specs=[ANY, ANY],
        out_shape=[out, out],
        scratch_shapes=[
            pltpu.VMEM((devices * ticks, rows, units), BF16),
            pltpu.VMEM((units, ticks * tokens), BF16),
            pltpu.VMEM((units, ticks * tokens), BF16),
            pltpu.VMEM((2, units, tile), BF16),
            pltpu.VMEM((2, units, tile), BF16),
            pltpu.SemaphoreType.DMA((2, 2)),
        ],
        compiler_params=PARAMS,
        cost_estimate=pl.CostEstimate(
            flops=4 * ticks * tokens * units * width, bytes_accessed=4 * units * width, transcendentals=0
        ),
        name="weight_grads",
    )(slots, saved, *rows_list, *weighted_list, *hid_list)


def hand_on_kernel(count, scalars, *refs):
    sums = refs[:count]
    base, loss, done_ref, next_ref, pick_ref = refs[count:]
    above, mine, top = scalars[0], scalars[1], scalars[2]
    total = sums[0][...].astype(F32)
    for ref in sums[1:]:
        total = total + ref[...].astype(F32)
    done = (base[above].astype(F32) + total).astype(BF16)
    done_ref[...] = done
    for b in range(base.shape[0]):
        from_above = jnp.where(above == b, done, base[b])
        next_ref[b] = jnp.where(top == 1, loss[b], from_above)
    pick_ref[...] = next_ref[mine]


def hand_on(sums, base, loss, scalars):
    rows, width = sums[0].shape
    chunk = jax.ShapeDtypeStruct((rows, width), BF16)
    return pl.pallas_call(
        functools.partial(hand_on_kernel, len(sums)),
        in_specs=[SMEM] + [VMEM] * (len(sums) + 2),
        out_specs=[VMEM] * 3,
        out_shape=[chunk, jax.ShapeDtypeStruct(base.shape, BF16), chunk],
        compiler_params=PARAMS,
        name="hand_on",
    )(scalars, *sums, base, loss)


def finish_kernel(count, ticks, picks, *refs):
    sums = refs[:count]
    incoming = refs[count : count + ticks]
    done = refs[count + ticks : count + 2 * ticks - 1]
    passed = refs[-1]
    for t in range(ticks):
        for b in range(passed.shape[1]):
            passed[t, b] = incoming[t][b]
        if t < ticks - 1:
            passed[t, picks[t]] = done[t][...]
    total = sums[0][...].astype(F32)
    for ref in sums[1:]:
        total = total + ref[...].astype(F32)
    last = picks[ticks - 1]
    passed[ticks - 1, last] = (incoming[ticks - 1][last].astype(F32) + total).astype(BF16)


def finish(sums, incoming, done, picks):
    ticks = len(incoming)
    return pl.pallas_call(
        functools.partial(finish_kernel, len(sums), ticks),
        in_specs=[SMEM] + [VMEM] * (len(sums) + 2 * ticks - 1),
        out_specs=VMEM,
        out_shape=jax.ShapeDtypeStruct((ticks,) + incoming[0].shape, BF16),
        compiler_params=PARAMS,
        name="finish",
    )(picks, *sums, *incoming, *done)


def per_device(
    sections, devices, w_in, w_out, input_stash, hidden_stash, gate_stash, block_pick, slot_order, arriving, loss_grads
):
    ticks = slot_order.shape[1]
    rows = arriving.shape[2]
    inner = 2 ** ((devices.bit_length() - 1) // 2)
    outer = devices // inner
    me = lax.axis_index("dp")
    top = (lax.axis_index("section") == sections - 1).astype(jnp.int32)

    def swap(value, step):
        return lax.ppermute(value, "dp", [(i, i ^ step) for i in range(devices)])

    def shift(value, distance, step=0):
        route = [
            (s * devices + i, (s + distance) % sections * devices + (i ^ step))
            for s in range(sections)
            for i in range(devices)
        ]
        return lax.ppermute(value, ("section", "dp"), route)

    def gather(own):
        chunks = {0: own}
        for a in range(outer - 1, 0, -1):
            chunks[a * inner] = swap(own, a * inner)
        for a in range(outer):
            for b in range(1, inner):
                chunks[a * inner + b] = swap(chunks[a * inner], b)
        return [chunks[k] for k in range(devices)]

    def reduce_inner(parts):
        sums = {}
        for a in range(outer - 1, -1, -1):
            got = [swap(parts[a * inner + b], b).astype(F32) for b in range(1, inner)]
            sums[a] = sum(got, parts[a * inner].astype(F32)).astype(BF16)
        return sums

    slots = slot_order[0]
    picks = jnp.stack(
        [
            sum(jnp.where(slots[t] == p, block_pick[0, p], 0) for p in range(ticks))
            for t in range(ticks)
        ]
    )
    own = sum(
        jnp.where(picks[0] == b, arriving[0, b], jnp.zeros((), BF16)) for b in range(arriving.shape[1])
    )
    hidden = hidden_stash[0].reshape(ticks, devices, rows, -1)
    gates = gate_stash[0].reshape(ticks, devices, rows, 1)

    z_groups = [[a * inner + b for a in range(outer)] for b in range(inner)]
    x_groups = [[a * inner + b for b in range(inner)] for a in range(outer)]
    saved = lax.all_gather(input_stash[0], "dp", axis_index_groups=z_groups)
    saved = lax.all_gather(saved, "dp", axis_index_groups=x_groups)
    saved = saved.reshape(ticks * devices * rows, -1)

    above_picks = shift(picks, -1)
    incoming = [arriving[0]]
    done = []
    gate_parts = []
    rows_list, weighted_list, hid_list = [], [], []
    for t in range(ticks):
        chunks = gather(own)
        results = expert(
            chunks, w_out[0], w_in[0], hidden, gates, jnp.stack([me.astype(jnp.int32), slots[t]]), inner
        )
        parts = results[:devices]
        rows_list.append(results[devices])
        weighted_list.append(results[devices + 1])
        hid_list.append(results[devices + 2])
        gate_parts.append(results[devices + 3])
        sums = reduce_inner(parts)
        if t < ticks - 1:
            base = shift(incoming[t], -1)
            sums = [shift(sums[a], -1, a * inner) for a in range(outer - 1, -1, -1)]
            above_done, following, own = hand_on(
                sums, base, loss_grads[t], jnp.stack([above_picks[t], picks[t + 1], top])
            )
            done.append(shift(above_done, 1))
            incoming.append(following)
        else:
            sums = [swap(sums[a], a * inner) for a in range(outer - 1, 0, -1)] + [sums[0]]
    grad_in, grad_out = weight_grads(slot_order, saved, rows_list, weighted_list, hid_list)
    gate = jnp.stack(gate_parts).reshape(ticks, devices * rows)
    step = 1
    while step < devices:
        gate = gate + swap(gate, step)
        step *= 2
    gate = jnp.stack([sum(jnp.where(slots[t] == p, gate[t], 0.0) for t in range(ticks)) for p in range(ticks)])
    passed = finish(sums, incoming, done, picks)
    return passed[None], grad_in[None], grad_out[None], gate[None]


def solution(mesh):
    placed = (
        P("section", "dp", None),
        P("section", "dp", None),
        P("section", None, "dp", None),
        P("section", None, None, "dp"),
        P("section", None, None),
        P("section", None),
        P("section", None),
        P("section", None, "dp", None),
        P(None, None, "dp", None),
    )
    return jax.shard_map(
        functools.partial(per_device, mesh.shape["section"], mesh.shape["dp"]),
        mesh=mesh,
        in_specs=placed,
        out_specs=(
            P("section", None, None, "dp", None),
            P("section", "dp", None),
            P("section", "dp", None),
            P("section", None, None),
        ),
        check_vma=False,
    )
```

```python
import functools

import jax
import jax.numpy as jnp
from jax import lax
from jax.experimental import pallas as pl
from jax.experimental.pallas import tpu as pltpu
from jax.sharding import PartitionSpec as P

BF16 = jnp.bfloat16
F32 = jnp.float32
VMEM = pl.BlockSpec(memory_space=pltpu.VMEM)
SMEM = pl.BlockSpec(memory_space=pltpu.SMEM)
ANY = pl.BlockSpec(memory_space=pl.ANY)
HBM = pl.BlockSpec(memory_space=pltpu.HBM)
PARAMS = pltpu.CompilerParams(vmem_limit_bytes=16 * 2**20)


def in_hbm(array):
    return pltpu.with_memory_space_constraint(array, pltpu.HBM)


def column_tile(width):
    return 512 if width % 512 == 0 else width


def pick_kernel(slot_hbm, block_hbm, arriving, own_ref, info_ref, slot_order, block_pick, blocks, sems):
    ticks = slot_hbm.shape[1]
    copies = [
        pltpu.make_async_copy(source, target, sems.at[i])
        for i, (source, target) in enumerate(((slot_hbm, slot_order), (block_hbm, block_pick), (arriving, blocks)))
    ]
    for copy in copies:
        copy.start()
    for copy in copies:
        copy.wait()
    for t in range(ticks):
        info_ref[t] = slot_order[0, t]
        info_ref[ticks + t] = block_pick[0, slot_order[0, t]]
    own_ref[...] = blocks[block_pick[0, slot_order[0, 0]]]


def pick(slot_order, block_pick, arriving):
    return pl.pallas_call(
        pick_kernel,
        in_specs=[HBM, HBM, HBM],
        out_specs=[VMEM, SMEM],
        out_shape=[
            jax.ShapeDtypeStruct(arriving.shape[1:], BF16),
            jax.ShapeDtypeStruct((2 * slot_order.shape[1],), jnp.int32),
        ],
        scratch_shapes=[
            pltpu.SMEM(slot_order.shape, jnp.int32),
            pltpu.SMEM(block_pick.shape, jnp.int32),
            pltpu.VMEM(arriving.shape, BF16),
            pltpu.SemaphoreType.DMA((3,)),
        ],
        compiler_params=PARAMS,
        name="pick",
    )(in_hbm(slot_order), in_hbm(block_pick), in_hbm(arriving))


PIECES = 4


def as_column(row):
    return jnp.broadcast_to(row, (128, row.shape[1])).T[:, :1]


def as_row(column):
    return jnp.broadcast_to(column, (column.shape[0], 128)).T[:1]


def prepare_kernel(devices, info, hidden, gates, w_out, w_in, out_v, in_v, active_ref, scale_ref, weighted_ref, scales, sems):
    units = w_out.shape[0]
    piece = units // PIECES
    copies = []
    for w, (source, target) in enumerate(((w_out, out_v), (w_in, in_v))):
        for p in range(PIECES):
            rows = pl.ds(p * piece, piece)
            copies.append(pltpu.make_async_copy(source.at[rows], target.at[rows], sems.at[w, p]))
            copies[-1].start()
    ticks, _, rows, _ = hidden.shape
    me = lax.axis_index("dp")
    for t in range(ticks):
        slot = info[t]
        scales[...] = as_column(gates[0, pl.ds(slot, 1), :]).reshape(devices, rows, 1)
        for k in range(devices):
            peer = me ^ k
            own = pl.ds(k * rows, rows)
            active = jnp.maximum(hidden[slot, peer].astype(F32), 0.0)
            scale = scales[peer]
            active_ref[t, own, :] = active
            scale_ref[t, own, :] = scale
            weighted_ref[t, own, :] = (active * scale).astype(BF16)
    for copy in copies:
        copy.wait()


def prepare(info, hidden, gates, w_out, w_in):
    ticks, devices, rows, units = hidden.shape
    tokens = devices * rows
    return pl.pallas_call(
        functools.partial(prepare_kernel, devices),
        in_specs=[SMEM, VMEM, VMEM, HBM, HBM],
        out_specs=[VMEM] * 5,
        out_shape=[
            pltpu.VMEM(w_out.shape, BF16),
            pltpu.VMEM(w_in.shape, BF16),
            jax.ShapeDtypeStruct((ticks, tokens, units), F32),
            jax.ShapeDtypeStruct((ticks, tokens, 1), F32),
            jax.ShapeDtypeStruct((ticks, tokens, units), BF16),
        ],
        scratch_shapes=[pltpu.VMEM((devices, rows, 1), F32), pltpu.SemaphoreType.DMA((2, PIECES))],
        compiler_params=PARAMS,
        cost_estimate=pl.CostEstimate(
            flops=2 * ticks * tokens * units, bytes_accessed=4 * w_out.size, transcendentals=0
        ),
        name="prepare",
    )(info, hidden, gates, in_hbm(w_out), in_hbm(w_in))


def expert_kernel(devices, inner, tick, inputs, *refs):
    chunks = refs[:inputs]
    w_out, w_in, active_ref, scale_ref = refs[inputs : inputs + 4]
    parts = refs[inputs + 4 : -4]
    rows_ref, hid_ref, gate_ref, sums = refs[-4:]
    tokens = rows_ref.shape[0]
    rows = tokens // devices
    start = 0
    for chunk in chunks:
        rows_ref[pl.ds(start, chunk.shape[0]), :] = chunk[...]
        start += chunk.shape[0]
    upstream = lax.dot_general(
        rows_ref[...], w_out[...], (((1,), (1,)), ((), ())), preferred_element_type=F32
    )
    active = active_ref[tick]
    hid_grad = jnp.where(active > 0, upstream * scale_ref[tick], 0.0).astype(BF16)
    width = w_in.shape[1]
    tile = column_tile(width)
    for first in range(0, width, tile):
        cols = pl.ds(first, tile)
        part = jnp.dot(hid_grad, w_in[:, cols], preferred_element_type=F32).astype(BF16)
        start = 0
        for ref in parts:
            ref[:, cols] = part[start : start + ref.shape[0]]
            start += ref.shape[0]
    gate_sum = jnp.sum(active * upstream, axis=1, keepdims=True)
    outer = devices // inner
    me = lax.axis_index("dp")
    for k in range(devices):
        sums[me ^ k] = gate_sum[k * rows : (k + 1) * rows]
        hid_ref[k % inner * outer + k // inner] = hid_grad[k * rows : (k + 1) * rows]
    gate_ref[...] = as_row(sums[...].reshape(tokens, 1))


def expert(tick, chunks, w_out, w_in, active, scale, devices, inner):
    units, width = w_out.shape
    tokens = active.shape[1]
    rows = tokens // devices
    sizes = [inner * rows] * 2 + [rows] * (devices - 2 * inner)
    return pl.pallas_call(
        functools.partial(expert_kernel, devices, inner, tick, len(chunks)),
        in_specs=[VMEM] * (len(chunks) + 4),
        out_specs=[VMEM] * (len(sizes) + 3),
        out_shape=[jax.ShapeDtypeStruct((size, width), BF16) for size in sizes]
        + [
            jax.ShapeDtypeStruct((tokens, width), BF16),
            jax.ShapeDtypeStruct((devices, rows, units), BF16),
            jax.ShapeDtypeStruct((1, tokens), F32),
        ],
        scratch_shapes=[pltpu.VMEM((devices, rows, 1), F32)],
        compiler_params=PARAMS,
        cost_estimate=pl.CostEstimate(
            flops=4 * tokens * units * width, bytes_accessed=2 * 2**20, transcendentals=0
        ),
        name="expert_tick",
    )(*chunks, w_out, w_in, active, scale)


def product_by_columns(left_ref, right_of, out, first, last, bufs, sems):
    tile = bufs.shape[2]
    copies = []
    for step, start in enumerate(range(first, last, tile)):
        buf = step % 2
        if step >= 2:
            copies[step - 2].wait()
        bufs[buf] = jnp.dot(left_ref[...], right_of(start, tile), preferred_element_type=F32).astype(BF16)
        copies.append(pltpu.make_async_copy(bufs.at[buf], out.at[:, pl.ds(start, tile)], sems.at[buf]))
        copies[-1].start()
    for copy in copies[max(len(copies) - 2, 0) :]:
        copy.wait()


def grad_out_kernel(first, last, weighted, *refs):
    ticks, tokens, _ = weighted.shape
    rows_refs = refs[:ticks]
    out, left, bufs, sems = refs[-4:]
    for t in range(ticks):
        left[:, t * tokens : (t + 1) * tokens] = weighted[t].T

    def right_of(start, size):
        return jnp.concatenate([ref[:, pl.ds(start, size)] for ref in rows_refs], axis=0)

    product_by_columns(left, right_of, out, first, last, bufs, sems)


def grad_in_kernel(ticks, inner, pieces, first, last, info, *refs):
    hid_refs = refs[:ticks]
    groups = max(group for slot in pieces for _, _, group, _ in slot) + 1
    saved = refs[ticks : ticks + groups * inner]
    out, hid_all, left, bufs, sems = refs[-5:]
    devices, rows, units = hid_refs[0].shape
    tokens = devices * rows
    for t in range(ticks):
        hid_all[info[t]] = hid_refs[t][...]
    left[...] = hid_all[...].reshape(ticks * tokens, units).T

    def right_of(start, size):
        found = []
        for slot in pieces:
            for begin, end, group, offset in slot:
                if begin <= start < end:
                    cols = pl.ds(offset + start - begin, size)
                    for ref in saved[group * inner : (group + 1) * inner]:
                        found.append(ref[:, :, cols].reshape(-1, size))
        return jnp.concatenate(found, axis=0)

    product_by_columns(left, right_of, out, first, last, bufs, sems)


def grad_call(kernel, shape, depth, columns, args, name, scratch=(), scalars=0, onto=None):
    units, width = shape
    tile = column_tile(columns[1] - columns[0])
    more = [] if onto is None else [onto]
    return pl.pallas_call(
        kernel,
        in_specs=[SMEM] * scalars + [VMEM] * (len(args) - scalars) + [ANY] * len(more),
        out_specs=ANY,
        out_shape=jax.ShapeDtypeStruct(shape, BF16),
        scratch_shapes=list(scratch)
        + [
            pltpu.VMEM((units, depth), BF16),
            pltpu.VMEM((2, units, tile), BF16),
            pltpu.SemaphoreType.DMA((2,)),
        ],
        input_output_aliases={len(args): 0} if more else {},
        compiler_params=PARAMS,
        cost_estimate=pl.CostEstimate(
            flops=2 * depth * units * (columns[1] - columns[0]),
            bytes_accessed=2 * units * (columns[1] - columns[0]),
            transcendentals=0,
        ),
        name=name,
    )(*args, *more)


def total_of(sums, rows):
    total = sums[0][:rows].astype(F32)
    for ref in sums[1:]:
        total = total + ref[:rows].astype(F32)
    return total


def hand_on_kernel(tick, ticks, top, info, above_info, *refs):
    sums = refs[:-5]
    base, loss, done_ref, next_ref, pick_ref = refs[-5:]
    above, mine = above_info[ticks + tick], info[ticks + tick + 1]
    is_top = lax.axis_index("section") == top
    total = total_of(sums, done_ref.shape[0])
    done = (base[above].astype(F32) + total).astype(BF16)
    done_ref[...] = done
    for b in range(base.shape[0]):
        from_above = jnp.where(above == b, done, base[b])
        next_ref[b] = jnp.where(is_top, loss[b], from_above)
    pick_ref[...] = next_ref[mine]


def hand_on(tick, ticks, top, info, above_info, sums, base, loss):
    chunk = jax.ShapeDtypeStruct(base.shape[1:], BF16)
    return pl.pallas_call(
        functools.partial(hand_on_kernel, tick, ticks, top),
        in_specs=[SMEM] * 2 + [VMEM] * (len(sums) + 2),
        out_specs=[VMEM] * 3,
        out_shape=[chunk, jax.ShapeDtypeStruct(base.shape, BF16), chunk],
        compiler_params=PARAMS,
        name="hand_on",
    )(info, above_info, *sums, base, loss)


def finish_kernel(count, ticks, inner, info, *refs):
    sums = refs[:count]
    incoming = refs[count : count + ticks]
    done = refs[count + ticks : count + 2 * ticks - 1]
    gates = refs[count + 2 * ticks - 1 : -3]
    passed, gate_ref, ordered = refs[-3:]
    for t in range(ticks):
        for b in range(passed.shape[1]):
            passed[t, b] = incoming[t][b]
        if t < ticks - 1:
            passed[t, info[ticks + t]] = done[t][...]
    total = total_of(sums, passed.shape[2])
    last = info[2 * ticks - 1]
    passed[ticks - 1, last] = (incoming[ticks - 1][last].astype(F32) + total).astype(BF16)
    own = lax.axis_index("dp") // inner
    for a, ref in enumerate(gates):
        ordered[own ^ a] = ref[...]
    gate = ordered[0]
    for a in range(1, len(gates)):
        gate = gate + ordered[a]
    for t in range(ticks):
        gate_ref[info[t]] = gate[t : t + 1]


def finish(sums, incoming, done, gates, info, inner):
    ticks = len(incoming)
    return pl.pallas_call(
        functools.partial(finish_kernel, len(sums), ticks, inner),
        in_specs=[SMEM] + [VMEM] * (len(sums) + 2 * ticks - 1 + len(gates)),
        out_specs=[VMEM, VMEM],
        out_shape=[
            jax.ShapeDtypeStruct((ticks,) + incoming[0].shape, BF16),
            jax.ShapeDtypeStruct((ticks, 1, gates[0].shape[1]), F32),
        ],
        scratch_shapes=[pltpu.VMEM((len(gates),) + gates[0].shape, F32)],
        compiler_params=PARAMS,
        name="finish",
    )(info, *sums, *incoming, *done, *gates)


def after(value, *others):
    return lax.optimization_barrier((value,) + others)[0]


def per_device(
    sections, devices, w_in, w_out, input_stash, hidden_stash, gate_stash, block_pick, slot_order, arriving, loss_grads
):
    ticks = slot_order.shape[1]
    _, units, width = w_out.shape
    rows = arriving.shape[2]
    tokens = devices * rows
    half = width // 2
    inner = 2 ** ((devices.bit_length() - 1) // 2)
    outer = devices // inner
    far = list(range(outer - 1, 1, -1))

    def swap(value, step):
        return lax.ppermute(value, "dp", [(i, i ^ step) for i in range(devices)])

    def shift(value, distance, step=0):
        route = [
            (s * devices + i, (s + distance) % sections * devices + (i ^ step))
            for s in range(sections)
            for i in range(devices)
        ]
        return lax.ppermute(value, ("section", "dp"), route)

    def along_inner(own):
        return [own] + [swap(own, b) for b in range(1, inner)]

    own, info = pick(slot_order, block_pick, arriving[0])
    hidden = hidden_stash[0].reshape(ticks, devices, rows, -1)
    stash_groups = [
        jnp.concatenate([input_stash[0, p] for p in range(ticks - 1)], axis=1),
        input_stash[0, -1],
    ]
    pieces = [[(0, width, 0, p * width)] for p in range(ticks - 1)]
    pieces.append([(0, width, 1, 0)])

    incoming = [arriving[0]]
    done = []
    gate_parts = []
    rows_list, hid_list, saved = [], [], []
    for t in range(ticks):
        last = t == ticks - 1
        column = {a: swap(own, a * inner) for a in far}
        mine = along_inner(own)
        if not last:
            above_info = shift(after(info, own), -1)
            base = shift(after(incoming[t], own), -1)
        near = swap(jnp.concatenate(mine), inner)
        if t == 0:
            out_v, in_v, active, scale, weighted = prepare(
                after(info, mine[-1]), hidden, gate_stash, w_out[0], w_in[0]
            )
            column[far[-1]] = after(column[far[-1]], active)
        chunks = {a: along_inner(column[a]) for a in far}
        stash = None
        if t == 0 or last:
            stash = after(stash_groups[int(last)], column[far[-1]])
            stash = [stash] + [swap(stash, a * inner) for a in range(1, outer)]
        if not last:
            near = after(near, above_info, base)
        results = expert(
            t,
            mine + [near] + [chunk for a in far[::-1] for chunk in chunks[a]],
            out_v,
            in_v,
            active,
            scale,
            devices,
            inner,
        )
        parts = results[:-3]
        rows_list.append(results[-3])
        hid_list.append(results[-2])
        gate_parts.append(results[-1])

        def send(value, step):
            return swap(value, step) if last else shift(value, -1, step)

        direct = send(parts[1], inner)
        kept = parts[0] if last else send(parts[0], 0)
        sums = {}
        for a in far:
            pieces_a = parts[2 + (a - 2) * inner :][:inner]
            got = [swap(pieces_a[b], b).astype(F32) for b in range(1, inner)]
            sums[a] = sum(got, pieces_a[0].astype(F32)).astype(BF16)
        crossing = [
            swap((kept[b * rows :][:rows].astype(F32) + direct[b * rows :][:rows].astype(F32)).astype(BF16), b)
            for b in range(1, inner)
        ]
        if stash is not None:
            stash = jnp.stack(stash)
            sums[far[0]], stash = lax.optimization_barrier((sums[far[0]], stash))
            saved += along_inner(after(stash, sums[far[-1]]))
        totals = [send(sums[a], a * inner) for a in far] + [kept, direct] + crossing
        if not last:
            above_done, following, own = hand_on(
                t, ticks, sections - 1, info, above_info, totals, base, loss_grads[t]
            )
            done.append(above_done)
            incoming.append(following)
    done = [shift(after(value, sums[far[-1]]), 1) for value in done]
    depth = ticks * tokens
    gate = after(jnp.concatenate(gate_parts), sums[far[0]])
    step = 1
    while step < inner:
        gate = gate + swap(gate, step)
        step *= 2
    rows_list[-1] = after(rows_list[-1], done[0])
    grad_out = grad_call(
        functools.partial(grad_out_kernel, 0, width),
        (units, width),
        depth,
        (0, width),
        (weighted, *rows_list),
        "grad_out",
    )
    gate = after(gate, totals[0])
    gates = [gate] + [swap(gate, a * inner) for a in range(1, outer)]
    grad_in = grad_call(
        functools.partial(grad_in_kernel, ticks, inner, pieces, 0, width),
        (units, width),
        depth,
        (0, width),
        (info, *hid_list[:-1], hid_list[-1], *saved),
        "grad_in",
        scratch=[pltpu.VMEM((ticks, devices, rows, units), BF16)],
        scalars=1,
    )
    passed, gate_grads = finish(
        totals, incoming, done, gates, info, inner
    )
    return passed[None], grad_in[None], grad_out[None], gate_grads.reshape(1, ticks, tokens)


def solution(mesh):
    placed = (
        P("section", "dp", None),
        P("section", "dp", None),
        P("section", None, "dp", None),
        P("section", None, None, "dp"),
        P("section", None, None),
        P("section", None),
        P("section", None),
        P("section", None, "dp", None),
        P(None, None, "dp", None),
    )
    return jax.shard_map(
        functools.partial(per_device, mesh.shape["section"], mesh.shape["dp"]),
        mesh=mesh,
        in_specs=placed,
        out_specs=(
            P("section", None, None, "dp", None),
            P("section", "dp", None),
            P("section", "dp", None),
            P("section", None, None),
        ),
        check_vma=False,
    )
```

```python
import functools

import jax
import jax.numpy as jnp
from jax import lax
from jax.experimental import pallas as pl
from jax.experimental.pallas import tpu as pltpu
from jax.sharding import PartitionSpec as P

BF16 = jnp.bfloat16
F32 = jnp.float32
VMEM = pl.BlockSpec(memory_space=pltpu.VMEM)
SMEM = pl.BlockSpec(memory_space=pltpu.SMEM)
ANY = pl.BlockSpec(memory_space=pl.ANY)
HBM = pl.BlockSpec(memory_space=pltpu.HBM)
PARAMS = pltpu.CompilerParams(vmem_limit_bytes=16 * 2**20)


def in_hbm(array):
    return pltpu.with_memory_space_constraint(array, pltpu.HBM)


def column_tile(width):
    return 512 if width % 512 == 0 else width


def pick_kernel(slot_hbm, block_hbm, arriving, own_ref, info_ref, slot_order, block_pick, blocks, sems):
    ticks = slot_hbm.shape[1]
    copies = [
        pltpu.make_async_copy(source, target, sems.at[i])
        for i, (source, target) in enumerate(((slot_hbm, slot_order), (block_hbm, block_pick), (arriving, blocks)))
    ]
    for copy in copies:
        copy.start()
    for copy in copies:
        copy.wait()
    for t in range(ticks):
        info_ref[t] = slot_order[0, t]
        info_ref[ticks + t] = block_pick[0, slot_order[0, t]]
    own_ref[...] = blocks[block_pick[0, slot_order[0, 0]]]


def pick(slot_order, block_pick, arriving):
    return pl.pallas_call(
        pick_kernel,
        in_specs=[HBM, HBM, HBM],
        out_specs=[VMEM, SMEM],
        out_shape=[
            jax.ShapeDtypeStruct(arriving.shape[1:], BF16),
            jax.ShapeDtypeStruct((2 * slot_order.shape[1],), jnp.int32),
        ],
        scratch_shapes=[
            pltpu.SMEM(slot_order.shape, jnp.int32),
            pltpu.SMEM(block_pick.shape, jnp.int32),
            pltpu.VMEM(arriving.shape, BF16),
            pltpu.SemaphoreType.DMA((3,)),
        ],
        compiler_params=PARAMS,
        name="pick",
    )(in_hbm(slot_order), in_hbm(block_pick), in_hbm(arriving))


PIECES = 4


def as_column(row):
    return jnp.broadcast_to(row, (128, row.shape[1])).T[:, :1]


def prepare_kernel(devices, info, hidden, gates, w_out, w_in, out_v, in_v, active_ref, scale_ref, weighted_ref, scales, sems):
    units = w_out.shape[0]
    piece = units // PIECES
    copies = []
    for w, (source, target) in enumerate(((w_out, out_v), (w_in, in_v))):
        for p in range(PIECES):
            rows = pl.ds(p * piece, piece)
            copies.append(pltpu.make_async_copy(source.at[rows], target.at[rows], sems.at[w, p]))
            copies[-1].start()
    ticks, _, rows, _ = hidden.shape
    me = lax.axis_index("dp")
    for t in range(ticks):
        slot = info[t]
        scales[...] = as_column(gates[0, pl.ds(slot, 1), :]).reshape(devices, rows, 1)
        for k in range(devices):
            peer = me ^ k
            own = pl.ds(k * rows, rows)
            active = jnp.maximum(hidden[slot, peer].astype(F32), 0.0)
            scale = scales[peer]
            active_ref[t, own, :] = active
            scale_ref[t, own, :] = scale
            weighted_ref[t, own, :] = (active * scale).astype(BF16)
    for copy in copies:
        copy.wait()


def prepare(info, hidden, gates, w_out, w_in):
    ticks, devices, rows, units = hidden.shape
    tokens = devices * rows
    return pl.pallas_call(
        functools.partial(prepare_kernel, devices),
        in_specs=[SMEM, VMEM, VMEM, HBM, HBM],
        out_specs=[VMEM] * 5,
        out_shape=[
            pltpu.VMEM(w_out.shape, BF16),
            pltpu.VMEM(w_in.shape, BF16),
            jax.ShapeDtypeStruct((ticks, tokens, units), F32),
            jax.ShapeDtypeStruct((ticks, tokens, 1), F32),
            jax.ShapeDtypeStruct((ticks, tokens, units), BF16),
        ],
        scratch_shapes=[pltpu.VMEM((devices, rows, 1), F32), pltpu.SemaphoreType.DMA((2, PIECES))],
        compiler_params=PARAMS,
        cost_estimate=pl.CostEstimate(
            flops=2 * ticks * tokens * units, bytes_accessed=4 * w_out.size, transcendentals=0
        ),
        name="prepare",
    )(info, hidden, gates, in_hbm(w_out), in_hbm(w_in))


def expert_kernel(devices, inner, tick, inputs, *refs):
    chunks = refs[:inputs]
    w_out, w_in, active_ref, scale_ref = refs[inputs : inputs + 4]
    parts = refs[inputs + 4 : -3]
    rows_ref, hid_ref, upstream_ref = refs[-3:]
    tokens = rows_ref.shape[0]
    rows = tokens // devices
    start = 0
    for chunk in chunks:
        rows_ref[pl.ds(start, chunk.shape[0]), :] = chunk[...]
        start += chunk.shape[0]
    upstream = lax.dot_general(
        rows_ref[...], w_out[...], (((1,), (1,)), ((), ())), preferred_element_type=F32
    )
    upstream_ref[...] = upstream
    hid_grad = jnp.where(active_ref[tick] > 0, upstream * scale_ref[tick], 0.0).astype(BF16)
    width = w_in.shape[1]
    tile = column_tile(width)
    for first in range(0, width, tile):
        cols = pl.ds(first, tile)
        part = jnp.dot(hid_grad, w_in[:, cols], preferred_element_type=F32).astype(BF16)
        start = 0
        for ref in parts:
            ref[:, cols] = part[start : start + ref.shape[0]]
            start += ref.shape[0]
    outer = devices // inner
    for k in range(devices):
        hid_ref[k % inner * outer + k // inner] = hid_grad[k * rows : (k + 1) * rows]


def gate_part_kernel(active, *refs):
    upstream = refs[:-2]
    gate_ref, products = refs[-2:]
    ticks, tokens, units = active.shape
    devices, rows, _ = products.shape
    me = lax.axis_index("dp")
    ones = jnp.ones((8, units), F32)
    for t in range(ticks):
        for k in range(devices):
            own = pl.ds(k * rows, rows)
            products[me ^ k] = active[t, own, :] * upstream[t][own, :]
        total = lax.dot_general(
            ones,
            products[...].reshape(tokens, units),
            (((1,), (1,)), ((), ())),
            precision=lax.Precision.HIGHEST,
            preferred_element_type=F32,
        )
        gate_ref[t : t + 1] = total[:1]


def gate_part(active, upstream, devices):
    ticks, tokens, units = active.shape
    return pl.pallas_call(
        gate_part_kernel,
        in_specs=[VMEM] * (ticks + 1),
        out_specs=VMEM,
        out_shape=jax.ShapeDtypeStruct((ticks, tokens), F32),
        scratch_shapes=[pltpu.VMEM((devices, tokens // devices, units), F32)],
        compiler_params=PARAMS,
        name="gate_part",
    )(active, *upstream)


def expert(tick, chunks, w_out, w_in, active, scale, devices, inner):
    units, width = w_out.shape
    tokens = active.shape[1]
    rows = tokens // devices
    sizes = [inner * rows] * 2 + [rows] * (devices - 2 * inner)
    return pl.pallas_call(
        functools.partial(expert_kernel, devices, inner, tick, len(chunks)),
        in_specs=[VMEM] * (len(chunks) + 4),
        out_specs=[VMEM] * (len(sizes) + 3),
        out_shape=[jax.ShapeDtypeStruct((size, width), BF16) for size in sizes]
        + [
            jax.ShapeDtypeStruct((tokens, width), BF16),
            jax.ShapeDtypeStruct((devices, rows, units), BF16),
            jax.ShapeDtypeStruct((tokens, units), F32),
        ],
        compiler_params=PARAMS,
        cost_estimate=pl.CostEstimate(
            flops=4 * tokens * units * width, bytes_accessed=2 * 2**20, transcendentals=0
        ),
        name="expert_tick",
    )(*chunks, w_out, w_in, active, scale)


def product_by_columns(left_ref, right_of, out, first, last, bufs, sems):
    tile = bufs.shape[2]
    copies = []
    for step, start in enumerate(range(first, last, tile)):
        bufs[step] = jnp.dot(left_ref[...], right_of(start, tile), preferred_element_type=F32).astype(BF16)
        copies.append(pltpu.make_async_copy(bufs.at[step], out.at[:, pl.ds(start, tile)], sems.at[step]))
        copies[-1].start()
    for copy in copies:
        copy.wait()


def grad_out_kernel(first, last, weighted, *refs):
    ticks, tokens, _ = weighted.shape
    rows_refs = refs[:ticks]
    out, left, bufs, sems = refs[-4:]
    for t in range(ticks):
        left[:, t * tokens : (t + 1) * tokens] = weighted[t].T

    def right_of(start, size):
        return jnp.concatenate([ref[:, pl.ds(start, size)] for ref in rows_refs], axis=0)

    product_by_columns(left, right_of, out, first, last, bufs, sems)


def grad_in_kernel(ticks, inner, pieces, first, last, info, *refs):
    hid_refs = refs[:ticks]
    groups = max(group for slot in pieces for _, _, group, _ in slot) + 1
    saved = refs[ticks : ticks + groups * inner]
    out, hid_all, left, bufs, sems = refs[-5:]
    devices, rows, units = hid_refs[0].shape
    tokens = devices * rows
    for t in range(ticks):
        hid_all[info[t]] = hid_refs[t][...]
    left[...] = hid_all[...].reshape(ticks * tokens, units).T

    def right_of(start, size):
        found = []
        for slot in pieces:
            for begin, end, group, offset in slot:
                if begin <= start < end:
                    cols = pl.ds(offset + start - begin, size)
                    for ref in saved[group * inner : (group + 1) * inner]:
                        found.append(ref[:, :, cols].reshape(-1, size))
        return jnp.concatenate(found, axis=0)

    product_by_columns(left, right_of, out, first, last, bufs, sems)


def grad_call(kernel, shape, depth, columns, args, name, scratch=(), scalars=0, onto=None):
    units, width = shape
    tile = column_tile(columns[1] - columns[0])
    steps = (columns[1] - columns[0]) // tile
    more = [] if onto is None else [onto]
    return pl.pallas_call(
        kernel,
        in_specs=[SMEM] * scalars + [VMEM] * (len(args) - scalars) + [ANY] * len(more),
        out_specs=ANY,
        out_shape=jax.ShapeDtypeStruct(shape, BF16),
        scratch_shapes=list(scratch)
        + [
            pltpu.VMEM((units, depth), BF16),
            pltpu.VMEM((steps, units, tile), BF16),
            pltpu.SemaphoreType.DMA((steps,)),
        ],
        input_output_aliases={len(args): 0} if more else {},
        compiler_params=PARAMS,
        cost_estimate=pl.CostEstimate(
            flops=2 * depth * units * (columns[1] - columns[0]),
            bytes_accessed=2 * units * (columns[1] - columns[0]),
            transcendentals=0,
        ),
        name=name,
    )(*args, *more)


def total_of(sums, rows):
    total = sums[0][:rows].astype(F32)
    for ref in sums[1:]:
        total = total + ref[:rows].astype(F32)
    return total


def hand_on_kernel(tick, ticks, top, info, above_info, *refs):
    sums = refs[:-5]
    base, loss, done_ref, next_ref, pick_ref = refs[-5:]
    above, mine = above_info[ticks + tick], info[ticks + tick + 1]
    is_top = lax.axis_index("section") == top
    total = total_of(sums, done_ref.shape[0])
    done = (base[above].astype(F32) + total).astype(BF16)
    done_ref[...] = done
    for b in range(base.shape[0]):
        from_above = jnp.where(above == b, done, base[b])
        next_ref[b] = jnp.where(is_top, loss[b], from_above)
    pick_ref[...] = next_ref[mine]


def hand_on(tick, ticks, top, info, above_info, sums, base, loss):
    chunk = jax.ShapeDtypeStruct(base.shape[1:], BF16)
    return pl.pallas_call(
        functools.partial(hand_on_kernel, tick, ticks, top),
        in_specs=[SMEM] * 2 + [VMEM] * (len(sums) + 2),
        out_specs=[VMEM] * 3,
        out_shape=[chunk, jax.ShapeDtypeStruct(base.shape, BF16), chunk],
        compiler_params=PARAMS,
        name="hand_on",
    )(info, above_info, *sums, base, loss)


def finish_kernel(count, ticks, inner, info, *refs):
    sums = refs[:count]
    incoming = refs[count : count + ticks]
    done = refs[count + ticks : count + 2 * ticks - 1]
    gates = refs[count + 2 * ticks - 1 : -3]
    passed, gate_ref, ordered = refs[-3:]
    for t in range(ticks):
        for b in range(passed.shape[1]):
            passed[t, b] = incoming[t][b]
        if t < ticks - 1:
            passed[t, info[ticks + t]] = done[t][...]
    total = total_of(sums, passed.shape[2])
    last = info[2 * ticks - 1]
    passed[ticks - 1, last] = (incoming[ticks - 1][last].astype(F32) + total).astype(BF16)
    own = lax.axis_index("dp") // inner
    for a, ref in enumerate(gates):
        ordered[own ^ a] = ref[...]
    gate = ordered[0]
    for a in range(1, len(gates)):
        gate = gate + ordered[a]
    for t in range(ticks):
        gate_ref[info[t]] = gate[t : t + 1]


def finish(sums, incoming, done, gates, info, inner):
    ticks = len(incoming)
    return pl.pallas_call(
        functools.partial(finish_kernel, len(sums), ticks, inner),
        in_specs=[SMEM] + [VMEM] * (len(sums) + 2 * ticks - 1 + len(gates)),
        out_specs=[VMEM, VMEM],
        out_shape=[
            jax.ShapeDtypeStruct((ticks,) + incoming[0].shape, BF16),
            jax.ShapeDtypeStruct((ticks, 1, gates[0].shape[1]), F32),
        ],
        scratch_shapes=[pltpu.VMEM((len(gates),) + gates[0].shape, F32)],
        compiler_params=PARAMS,
        name="finish",
    )(info, *sums, *incoming, *done, *gates)


def after(value, *others):
    return lax.optimization_barrier((value,) + others)[0]


def per_device(
    sections, devices, w_in, w_out, input_stash, hidden_stash, gate_stash, block_pick, slot_order, arriving, loss_grads
):
    ticks = slot_order.shape[1]
    _, units, width = w_out.shape
    rows = arriving.shape[2]
    tokens = devices * rows
    half = width // 2
    inner = 2 ** ((devices.bit_length() - 1) // 2)
    outer = devices // inner
    far = list(range(outer - 1, 1, -1))

    def swap(value, step):
        return lax.ppermute(value, "dp", [(i, i ^ step) for i in range(devices)])

    def shift(value, distance, step=0):
        route = [
            (s * devices + i, (s + distance) % sections * devices + (i ^ step))
            for s in range(sections)
            for i in range(devices)
        ]
        return lax.ppermute(value, ("section", "dp"), route)

    def along_inner(own):
        return [own] + [swap(own, b) for b in range(1, inner)]

    own, info = pick(slot_order, block_pick, arriving[0])
    hidden = hidden_stash[0].reshape(ticks, devices, rows, -1)
    stash_groups = [
        jnp.concatenate([input_stash[0, p] for p in range(ticks - 1)], axis=1),
        input_stash[0, -1],
    ]
    pieces = [[(0, width, 0, p * width)] for p in range(ticks - 1)]
    pieces.append([(0, width, 1, 0)])

    incoming = [arriving[0]]
    done = []
    gate_parts = []
    rows_list, hid_list, saved = [], [], []
    for t in range(ticks):
        last = t == ticks - 1
        column = {a: swap(own, a * inner) for a in far}
        mine = along_inner(own)
        if not last:
            above_info = shift(after(info, own), -1)
            base = shift(after(incoming[t], own), -1)
        near = swap(jnp.concatenate(mine), inner)
        if t == 0:
            out_v, in_v, active, scale, weighted = prepare(
                after(info, mine[-1]), hidden, gate_stash, w_out[0], w_in[0]
            )
            column[far[-1]] = after(column[far[-1]], active)
        if t > 0:
            column[far[-1]] = after(column[far[-1]], saved[-1])
        chunks = {a: along_inner(column[a]) for a in far}
        stash = None
        if t == 0 or last:
            stash = after(stash_groups[int(last)], column[far[-1]])
            stash = [stash] + [swap(stash, a * inner) for a in range(1, outer)]
        if not last:
            near = after(near, above_info, base)
        results = expert(
            t,
            mine + [near] + [chunk for a in far[::-1] for chunk in chunks[a]],
            out_v,
            in_v,
            active,
            scale,
            devices,
            inner,
        )
        parts = results[:-3]
        rows_list.append(results[-3])
        hid_list.append(results[-2])
        gate_parts.append(results[-1])

        def send(value, step):
            return swap(value, step) if last else shift(value, -1, step)

        direct = send(parts[1], inner)
        kept = parts[0] if last else send(parts[0], 0)
        sums = {}
        for a in far:
            pieces_a = parts[2 + (a - 2) * inner :][:inner]
            got = [swap(pieces_a[b], b).astype(F32) for b in range(1, inner)]
            sums[a] = sum(got, pieces_a[0].astype(F32)).astype(BF16)
        if last:
            gate = gate_part(active, gate_parts, devices)
            step = 1
            while step < inner:
                gate = gate + swap(gate, step)
                step *= 2
        crossing = [
            swap((kept[b * rows :][:rows].astype(F32) + direct[b * rows :][:rows].astype(F32)).astype(BF16), b)
            for b in range(1, inner)
        ]
        if stash is not None:
            stash = jnp.stack(stash)
            sums[far[0]], stash = lax.optimization_barrier((sums[far[0]], stash))
            late = after(stash, sums[far[-1]])
            if last:
                saved += along_inner(after(late, gate))
        totals = [send(sums[a], a * inner) for a in far] + [kept, direct] + crossing
        if not last:
            above_done, following, own = hand_on(
                t, ticks, sections - 1, info, above_info, totals, base, loss_grads[t]
            )
            done.append(above_done)
            incoming.append(following)
            saved += along_inner(after(late, own))
    done = [shift(after(value, sums[far[-1]]), 1) for value in done]
    depth = ticks * tokens
    rows_list[-1] = after(rows_list[-1], done[0])
    grad_out = grad_call(
        functools.partial(grad_out_kernel, 0, width),
        (units, width),
        depth,
        (0, width),
        (weighted, *rows_list),
        "grad_out",
    )
    gate = after(gate, direct)
    gates = [gate] + [swap(gate, a * inner) for a in range(1, outer)]
    grad_in = grad_call(
        functools.partial(grad_in_kernel, ticks, inner, pieces, 0, width),
        (units, width),
        depth,
        (0, width),
        (info, *hid_list[:-1], hid_list[-1], *saved),
        "grad_in",
        scratch=[pltpu.VMEM((ticks, devices, rows, units), BF16)],
        scalars=1,
    )
    passed, gate_grads = finish(
        totals, incoming, done, gates, info, inner
    )
    return passed[None], grad_in[None], grad_out[None], gate_grads.reshape(1, ticks, tokens)


def solution(mesh):
    placed = (
        P("section", "dp", None),
        P("section", "dp", None),
        P("section", None, "dp", None),
        P("section", None, None, "dp"),
        P("section", None, None),
        P("section", None),
        P("section", None),
        P("section", None, "dp", None),
        P(None, None, "dp", None),
    )
    return jax.shard_map(
        functools.partial(per_device, mesh.shape["section"], mesh.shape["dp"]),
        mesh=mesh,
        in_specs=placed,
        out_specs=(
            P("section", None, None, "dp", None),
            P("section", "dp", None),
            P("section", "dp", None),
            P("section", None, None),
        ),
        check_vma=False,
    )
```

```python
import functools

import jax
import jax.numpy as jnp
from jax import lax
from jax.experimental import pallas as pl
from jax.experimental.pallas import tpu as pltpu
from jax.sharding import PartitionSpec as P

BF16 = jnp.bfloat16
F32 = jnp.float32
VMEM = pl.BlockSpec(memory_space=pltpu.VMEM)
SMEM = pl.BlockSpec(memory_space=pltpu.SMEM)
ANY = pl.BlockSpec(memory_space=pl.ANY)
HBM = pl.BlockSpec(memory_space=pltpu.HBM)
PARAMS = pltpu.CompilerParams(vmem_limit_bytes=16 * 2**20)


def in_hbm(array):
    return pltpu.with_memory_space_constraint(array, pltpu.HBM)


def column_tile(width):
    return 512 if width % 512 == 0 else width


def pick_kernel(slot_hbm, block_hbm, arriving, own_ref, info_ref, slot_order, block_pick, blocks, sems):
    ticks = slot_hbm.shape[1]
    copies = [
        pltpu.make_async_copy(source, target, sems.at[i])
        for i, (source, target) in enumerate(((slot_hbm, slot_order), (block_hbm, block_pick), (arriving, blocks)))
    ]
    for copy in copies:
        copy.start()
    for copy in copies:
        copy.wait()
    for t in range(ticks):
        info_ref[t] = slot_order[0, t]
        info_ref[ticks + t] = block_pick[0, slot_order[0, t]]
    own_ref[...] = blocks[block_pick[0, slot_order[0, 0]]]


def pick(slot_order, block_pick, arriving):
    return pl.pallas_call(
        pick_kernel,
        in_specs=[HBM, HBM, HBM],
        out_specs=[VMEM, SMEM],
        out_shape=[
            jax.ShapeDtypeStruct(arriving.shape[1:], BF16),
            jax.ShapeDtypeStruct((2 * slot_order.shape[1],), jnp.int32),
        ],
        scratch_shapes=[
            pltpu.SMEM(slot_order.shape, jnp.int32),
            pltpu.SMEM(block_pick.shape, jnp.int32),
            pltpu.VMEM(arriving.shape, BF16),
            pltpu.SemaphoreType.DMA((3,)),
        ],
        compiler_params=PARAMS,
        name="pick",
    )(in_hbm(slot_order), in_hbm(block_pick), in_hbm(arriving))


PIECES = 4


def as_column(row):
    return jnp.broadcast_to(row, (128, row.shape[1])).T[:, :1]


def prepare_kernel(
    devices, info, hidden_hbm, gates_hbm, w_out, w_in, out_v, in_v, active_ref, scale_ref, weighted_ref, hidden, gates, scales, sems, small_sems
):
    units = w_out.shape[0]
    piece = units // PIECES
    small = [
        pltpu.make_async_copy(hidden_hbm, hidden, small_sems.at[0]),
        pltpu.make_async_copy(gates_hbm, gates, small_sems.at[1]),
    ]
    for copy in small:
        copy.start()
    copies = []
    for w, (source, target) in enumerate(((w_out, out_v), (w_in, in_v))):
        for p in range(PIECES):
            rows = pl.ds(p * piece, piece)
            copies.append(pltpu.make_async_copy(source.at[rows], target.at[rows], sems.at[w, p]))
            copies[-1].start()
    ticks, _, rows, _ = hidden.shape
    me = lax.axis_index("dp")
    for copy in small:
        copy.wait()
    for t in range(ticks):
        slot = info[t]
        scales[...] = as_column(gates[0, pl.ds(slot, 1), :]).reshape(devices, rows, 1)
        for k in range(devices):
            peer = me ^ k
            own = pl.ds(k * rows, rows)
            active = jnp.maximum(hidden[slot, peer].astype(F32), 0.0)
            scale = scales[peer]
            active_ref[t, own, :] = active
            scale_ref[t, own, :] = scale
            weighted_ref[t, own, :] = (active * scale).astype(BF16)
    for copy in copies:
        copy.wait()


def prepare(info, hidden, gates, w_out, w_in):
    ticks, devices, rows, units = hidden.shape
    tokens = devices * rows
    return pl.pallas_call(
        functools.partial(prepare_kernel, devices),
        in_specs=[SMEM, HBM, HBM, HBM, HBM],
        out_specs=[VMEM] * 5,
        out_shape=[
            pltpu.VMEM(w_out.shape, BF16),
            pltpu.VMEM(w_in.shape, BF16),
            jax.ShapeDtypeStruct((ticks, tokens, units), F32),
            jax.ShapeDtypeStruct((ticks, tokens, 1), F32),
            jax.ShapeDtypeStruct((ticks, tokens, units), BF16),
        ],
        scratch_shapes=[
            pltpu.VMEM(hidden.shape, BF16),
            pltpu.VMEM(gates.shape, F32),
            pltpu.VMEM((devices, rows, 1), F32),
            pltpu.SemaphoreType.DMA((2, PIECES)),
            pltpu.SemaphoreType.DMA((2,)),
        ],
        compiler_params=PARAMS,
        cost_estimate=pl.CostEstimate(
            flops=2 * ticks * tokens * units, bytes_accessed=4 * w_out.size, transcendentals=0
        ),
        name="prepare",
    )(info, in_hbm(hidden), in_hbm(gates), in_hbm(w_out), in_hbm(w_in))


def expert_kernel(devices, inner, tick, inputs, *refs):
    chunks = refs[:inputs]
    w_out, w_in, active_ref, scale_ref = refs[inputs : inputs + 4]
    parts = refs[inputs + 4 : -4]
    rows_ref, hid_ref, upstream_ref, left_ref = refs[-4:]
    tokens = rows_ref.shape[0]
    rows = tokens // devices
    start = 0
    for chunk in chunks:
        rows_ref[pl.ds(start, chunk.shape[0]), :] = chunk[...]
        start += chunk.shape[0]
    upstream = lax.dot_general(
        rows_ref[...], w_out[...], (((1,), (1,)), ((), ())), preferred_element_type=F32
    )
    upstream_ref[...] = upstream
    hid_grad = jnp.where(active_ref[tick] > 0, upstream * scale_ref[tick], 0.0).astype(BF16)
    width = w_in.shape[1]
    tile = width // 2 if width % 256 == 0 else width
    outer = devices // inner
    for k in range(devices):
        hid_ref[k % inner * outer + k // inner] = hid_grad[k * rows : (k + 1) * rows]
    left_ref[...] = hid_grad

    @pl.loop(0, width // tile)
    def _(step):
        cols = pl.ds(pl.multiple_of(step * tile, tile), tile)
        part = jnp.dot(left_ref[...], w_in[:, cols], preferred_element_type=F32).astype(BF16)
        start = 0
        for ref in parts:
            ref[:, cols] = part[start : start + ref.shape[0]]
            start += ref.shape[0]


def gate_part_kernel(active, *refs):
    upstream = refs[:-2]
    gate_ref, products = refs[-2:]
    ticks, tokens, units = active.shape
    devices, rows, _ = products.shape
    me = lax.axis_index("dp")
    ones = jnp.ones((8, units), F32)
    for t in range(ticks):
        for k in range(devices):
            own = pl.ds(k * rows, rows)
            products[me ^ k] = active[t, own, :] * upstream[t][own, :]
        total = lax.dot_general(
            ones,
            products[...].reshape(tokens, units),
            (((1,), (1,)), ((), ())),
            precision=lax.Precision.HIGHEST,
            preferred_element_type=F32,
        )
        gate_ref[t : t + 1] = total[:1]


def gate_part(active, upstream, devices):
    ticks, tokens, units = active.shape
    return pl.pallas_call(
        gate_part_kernel,
        in_specs=[VMEM] * (ticks + 1),
        out_specs=VMEM,
        out_shape=jax.ShapeDtypeStruct((ticks, tokens), F32),
        scratch_shapes=[pltpu.VMEM((devices, tokens // devices, units), F32)],
        compiler_params=PARAMS,
        name="gate_part",
    )(active, *upstream)


def expert(tick, chunks, w_out, w_in, active, scale, devices, inner):
    units, width = w_out.shape
    tokens = active.shape[1]
    rows = tokens // devices
    sizes = [inner * rows] * 2 + [rows] * (devices - 2 * inner)
    return pl.pallas_call(
        functools.partial(expert_kernel, devices, inner, tick, len(chunks)),
        in_specs=[VMEM] * (len(chunks) + 4),
        out_specs=[VMEM] * (len(sizes) + 3),
        out_shape=[jax.ShapeDtypeStruct((size, width), BF16) for size in sizes]
        + [
            jax.ShapeDtypeStruct((tokens, width), BF16),
            jax.ShapeDtypeStruct((devices, rows, units), BF16),
            jax.ShapeDtypeStruct((tokens, units), F32),
        ],
        scratch_shapes=[pltpu.VMEM((tokens, units), BF16)],
        compiler_params=PARAMS,
        cost_estimate=pl.CostEstimate(
            flops=4 * tokens * units * width, bytes_accessed=2 * 2**20, transcendentals=0
        ),
        name="expert_tick",
    )(*chunks, w_out, w_in, active, scale)


def product_by_columns(left_ref, right_of, out, first, last, bufs, sems):
    tile = bufs.shape[2]
    copies = []
    for step, start in enumerate(range(first, last, tile)):
        bufs[step] = jnp.dot(left_ref[...], right_of(start, tile), preferred_element_type=F32).astype(BF16)
        copies.append(pltpu.make_async_copy(bufs.at[step], out.at[:, pl.ds(start, tile)], sems.at[step]))
        copies[-1].start()
    for copy in copies:
        copy.wait()


def grad_out_kernel(first, last, weighted, *refs):
    ticks, tokens, _ = weighted.shape
    rows_refs = refs[:ticks]
    out, left, bufs, sems = refs[-4:]
    for t in range(ticks):
        left[:, t * tokens : (t + 1) * tokens] = weighted[t].T

    def right_of(start, size):
        return jnp.concatenate([ref[:, pl.ds(start, size)] for ref in rows_refs], axis=0)

    product_by_columns(left, right_of, out, first, last, bufs, sems)


def grad_in_kernel(ticks, inner, pieces, first, last, info, *refs):
    hid_refs = refs[:ticks]
    groups = max(group for slot in pieces for _, _, group, _ in slot) + 1
    saved = refs[ticks : ticks + groups * inner]
    out, hid_all, left, bufs, sems = refs[-5:]
    devices, rows, units = hid_refs[0].shape
    tokens = devices * rows
    for t in range(ticks):
        hid_all[info[t]] = hid_refs[t][...]
    left[...] = hid_all[...].reshape(ticks * tokens, units).T

    def right_of(start, size):
        found = []
        for slot in pieces:
            for begin, end, group, offset in slot:
                if begin <= start < end:
                    cols = pl.ds(offset + start - begin, size)
                    for ref in saved[group * inner : (group + 1) * inner]:
                        found.append(ref[:, :, cols].reshape(-1, size))
        return jnp.concatenate(found, axis=0)

    product_by_columns(left, right_of, out, first, last, bufs, sems)


def grad_call(kernel, shape, depth, columns, args, name, scratch=(), scalars=0, onto=None):
    units, width = shape
    tile = column_tile(columns[1] - columns[0])
    steps = (columns[1] - columns[0]) // tile
    more = [] if onto is None else [onto]
    return pl.pallas_call(
        kernel,
        in_specs=[SMEM] * scalars + [VMEM] * (len(args) - scalars) + [ANY] * len(more),
        out_specs=ANY,
        out_shape=jax.ShapeDtypeStruct(shape, BF16),
        scratch_shapes=list(scratch)
        + [
            pltpu.VMEM((units, depth), BF16),
            pltpu.VMEM((steps, units, tile), BF16),
            pltpu.SemaphoreType.DMA((steps,)),
        ],
        input_output_aliases={len(args): 0} if more else {},
        compiler_params=PARAMS,
        cost_estimate=pl.CostEstimate(
            flops=2 * depth * units * (columns[1] - columns[0]),
            bytes_accessed=2 * units * (columns[1] - columns[0]),
            transcendentals=0,
        ),
        name=name,
    )(*args, *more)


def total_of(sums, rows):
    total = sums[0][:rows].astype(F32)
    for ref in sums[1:]:
        total = total + ref[:rows].astype(F32)
    return total


def hand_on_kernel(tick, ticks, top, info, above_info, *refs):
    sums = refs[:-5]
    base, loss, done_ref, next_ref, pick_ref = refs[-5:]
    above, mine = above_info[ticks + tick], info[ticks + tick + 1]
    is_top = lax.axis_index("section") == top
    total = total_of(sums, done_ref.shape[0])
    done = (base[above].astype(F32) + total).astype(BF16)
    done_ref[...] = done
    for b in range(base.shape[0]):
        from_above = jnp.where(above == b, done, base[b])
        next_ref[b] = jnp.where(is_top, loss[b], from_above)
    pick_ref[...] = next_ref[mine]


def hand_on(tick, ticks, top, info, above_info, sums, base, loss):
    chunk = jax.ShapeDtypeStruct(base.shape[1:], BF16)
    return pl.pallas_call(
        functools.partial(hand_on_kernel, tick, ticks, top),
        in_specs=[SMEM] * 2 + [VMEM] * (len(sums) + 2),
        out_specs=[VMEM] * 3,
        out_shape=[chunk, jax.ShapeDtypeStruct(base.shape, BF16), chunk],
        compiler_params=PARAMS,
        name="hand_on",
    )(info, above_info, *sums, base, loss)


def finish_kernel(count, ticks, inner, info, *refs):
    sums = refs[:count]
    incoming = refs[count : count + ticks]
    done = refs[count + ticks : count + 2 * ticks - 1]
    gates = refs[count + 2 * ticks - 1 : -3]
    passed, gate_ref, ordered = refs[-3:]
    for t in range(ticks):
        for b in range(passed.shape[1]):
            passed[t, b] = incoming[t][b]
        if t < ticks - 1:
            passed[t, info[ticks + t]] = done[t][...]
    total = total_of(sums, passed.shape[2])
    last = info[2 * ticks - 1]
    passed[ticks - 1, last] = (incoming[ticks - 1][last].astype(F32) + total).astype(BF16)
    own = lax.axis_index("dp") // inner
    for a, ref in enumerate(gates):
        ordered[own ^ a] = ref[...]
    gate = ordered[0]
    for a in range(1, len(gates)):
        gate = gate + ordered[a]
    for t in range(ticks):
        gate_ref[info[t]] = gate[t : t + 1]


def finish(sums, incoming, done, gates, info, inner):
    ticks = len(incoming)
    return pl.pallas_call(
        functools.partial(finish_kernel, len(sums), ticks, inner),
        in_specs=[SMEM] + [VMEM] * (len(sums) + 2 * ticks - 1 + len(gates)),
        out_specs=[VMEM, VMEM],
        out_shape=[
            jax.ShapeDtypeStruct((ticks,) + incoming[0].shape, BF16),
            jax.ShapeDtypeStruct((ticks, 1, gates[0].shape[1]), F32),
        ],
        scratch_shapes=[pltpu.VMEM((len(gates),) + gates[0].shape, F32)],
        compiler_params=PARAMS,
        name="finish",
    )(info, *sums, *incoming, *done, *gates)


def after(value, *others):
    return lax.optimization_barrier((value,) + others)[0]


def per_device(
    sections, devices, w_in, w_out, input_stash, hidden_stash, gate_stash, block_pick, slot_order, arriving, loss_grads
):
    ticks = slot_order.shape[1]
    _, units, width = w_out.shape
    rows = arriving.shape[2]
    tokens = devices * rows
    half = width // 2
    inner = 2 ** ((devices.bit_length() - 1) // 2)
    outer = devices // inner
    far = list(range(outer - 1, 1, -1))

    def swap(value, step):
        return lax.ppermute(value, "dp", [(i, i ^ step) for i in range(devices)])

    def shift(value, distance, step=0):
        route = [
            (s * devices + i, (s + distance) % sections * devices + (i ^ step))
            for s in range(sections)
            for i in range(devices)
        ]
        return lax.ppermute(value, ("section", "dp"), route)

    def along_inner(own):
        return [own] + [swap(own, b) for b in range(1, inner)]

    own, info = pick(slot_order, block_pick, arriving[0])
    hidden = hidden_stash[0].reshape(ticks, devices, rows, -1)
    stash_groups = [
        jnp.concatenate([input_stash[0, p] for p in range(ticks - 1)], axis=1),
        input_stash[0, -1],
    ]
    pieces = [[(0, width, 0, p * width)] for p in range(ticks - 1)]
    pieces.append([(0, width, 1, 0)])

    incoming = [arriving[0]]
    done = []
    gate_parts = []
    rows_list, hid_list, saved = [], [], []
    for t in range(ticks):
        last = t == ticks - 1
        column = {a: swap(own, a * inner) for a in far}
        mine = along_inner(own)
        if not last:
            above_info = shift(after(info, own), -1)
            base = shift(after(incoming[t], own), -1)
        near = swap(jnp.concatenate(mine), inner)
        if t == 0:
            out_v, in_v, active, scale, weighted = prepare(
                after(info, mine[-1]), hidden, gate_stash, w_out[0], w_in[0]
            )
            column[far[-1]] = after(column[far[-1]], active)
        if t > 0:
            column[far[-1]] = after(column[far[-1]], saved[-1])
        chunks = {a: along_inner(column[a]) for a in far}
        stash = None
        if t == 0 or last:
            stash = after(stash_groups[int(last)], column[far[-1]])
            stash = [stash] + [swap(stash, a * inner) for a in range(1, outer)]
        if not last:
            near = after(near, above_info, base)
        results = expert(
            t,
            mine + [near] + [chunk for a in far[::-1] for chunk in chunks[a]],
            out_v,
            in_v,
            active,
            scale,
            devices,
            inner,
        )
        parts = results[:-3]
        rows_list.append(results[-3])
        hid_list.append(results[-2])
        gate_parts.append(results[-1])

        def send(value, step):
            return swap(value, step) if last else shift(value, -1, step)

        direct = send(parts[1], inner)
        kept = parts[0] if last else send(parts[0], 0)
        sums = {}
        for a in far:
            pieces_a = parts[2 + (a - 2) * inner :][:inner]
            got = [swap(pieces_a[b], b).astype(F32) for b in range(1, inner)]
            sums[a] = sum(got, pieces_a[0].astype(F32)).astype(BF16)
        if last:
            gate = gate_part(active, gate_parts, devices)
            step = 1
            while step < inner:
                gate = gate + swap(gate, step)
                step *= 2
        crossing = [
            swap((kept[b * rows :][:rows].astype(F32) + direct[b * rows :][:rows].astype(F32)).astype(BF16), b)
            for b in range(1, inner)
        ]
        if stash is not None:
            stash = jnp.stack(stash)
            tie = far[0] if last else far[-1]
            sums[tie], stash = lax.optimization_barrier((sums[tie], stash))
            late = after(stash, sums[far[-1]])
            if last:
                saved += along_inner(after(late, gate))
        totals = [send(sums[a], a * inner) for a in far] + [kept, direct] + crossing
        if not last:
            above_done, following, own = hand_on(
                t, ticks, sections - 1, info, above_info, totals, base, loss_grads[t]
            )
            done.append(above_done)
            incoming.append(following)
            saved += along_inner(after(late, totals[1]))
    done = [shift(after(value, sums[far[-1]]), 1) for value in done]
    depth = ticks * tokens
    rows_list[-1] = after(rows_list[-1], done[0])
    grad_out = grad_call(
        functools.partial(grad_out_kernel, 0, width),
        (units, width),
        depth,
        (0, width),
        (weighted, *rows_list),
        "grad_out",
    )
    gate = after(gate, direct)
    gates = [gate] + [swap(gate, a * inner) for a in range(1, outer)]
    grad_in = grad_call(
        functools.partial(grad_in_kernel, ticks, inner, pieces, 0, width),
        (units, width),
        depth,
        (0, width),
        (info, *hid_list[:-1], hid_list[-1], *saved),
        "grad_in",
        scratch=[pltpu.VMEM((ticks, devices, rows, units), BF16)],
        scalars=1,
    )
    passed, gate_grads = finish(
        totals, incoming, done, gates, info, inner
    )
    return passed[None], grad_in[None], grad_out[None], gate_grads.reshape(1, ticks, tokens)


def solution(mesh):
    placed = (
        P("section", "dp", None),
        P("section", "dp", None),
        P("section", None, "dp", None),
        P("section", None, None, "dp"),
        P("section", None, None),
        P("section", None),
        P("section", None),
        P("section", None, "dp", None),
        P(None, None, "dp", None),
    )
    return jax.shard_map(
        functools.partial(per_device, mesh.shape["section"], mesh.shape["dp"]),
        mesh=mesh,
        in_specs=placed,
        out_specs=(
            P("section", None, None, "dp", None),
            P("section", "dp", None),
            P("section", "dp", None),
            P("section", None, None),
        ),
        check_vma=False,
    )
```
